512 devices in a mesh: dp: 8 (over y), ctx: 64 (over z, x, core).
Axes of the slice: x: 4, y: 8, z: 8, core: 2. Of those that a mesh axis runs over, the one named last changes fastest.
Arguments:
- query: bfloat16 [8, 16384, 1024], P('dp', 'ctx'), may hold values from -6 to 6
- keys: bfloat16 [8, 16384, 1024], P('dp', 'ctx'), may hold values from -6 to 6
- values: bfloat16 [8, 16384, 1024], P('dp', 'ctx'), may hold values from -6 to 6
- cotangent: bfloat16 [8, 16384, 1024], P('dp', 'ctx'), may hold values from -16 to 16
- out_weight: bfloat16 [1024, 1024], P('dp'), may hold values from -0.1875 to 0.1875
Outputs:
- query_grad: bfloat16 [8, 16384, 1024], P('dp', 'ctx')
- derivative_of_keys: bfloat16 [8, 16384, 1024], P('dp', 'ctx')
- derivative_of_values: bfloat16 [8, 16384, 1024], P('dp', 'ctx')
- weight_grad: float32 [1024, 1024], P(('dp', 'ctx'))
The draws below stay inside these ranges and needn't reach their ends.
All inputs are finite; a program needn't handle non-finite values.
Results may differ from the reference program's by a relative error of at most 0.015.
Values may be sent and summed in bfloat16 or wider, within the bound.
No kernel may reach another device: no remote copies, remote signals or barrier semaphores. Data moves between devices by JAX's collectives and lax.ppermute only.
A program may use at most 192 MiB of HBM per device.

```python
import math
import jax
import jax.numpy as jnp
from jax import lax

D = 1024
HEAD = 128
TOK_DEV = 256
HD = 1024
LENGTH = 16384
BATCH = 8


def strengthened(entries, key, source, target, parts, factor):
    owner, partner = [(jnp.arange(entries.shape[dim]) // (entries.shape[dim] // parts)).reshape([-1 if axis == dim else 1 for axis in range(entries.ndim)]) for dim in (source, target)]
    chosen = jax.random.permutation(key, parts)[partner]
    strong = (owner == chosen) | (owner == (partner + parts // 2) % parts)
    return jnp.where(strong, factor * entries, entries)


def levels(rng, shape, cuts, least, largest):
    loudness, own = 1.0, jax.random.fold_in(rng, 6)
    for position, parts in cuts:
        heights = jnp.exp(jax.random.uniform(jax.random.fold_in(own, position), (parts,), jnp.float32, least / len(cuts), largest / len(cuts)))
        loudness = loudness * jnp.repeat(heights, shape[position] // parts).reshape([-1 if axis == position else 1 for axis in range(len(shape))])
    return loudness


def bell_draw(rng, extent, spread, most, shards=(), held_as=jnp.bfloat16):
    drawn = jax.random.normal(rng, extent, jnp.float32) * spread
    if len(shards) > 0:
        drawn = levels(rng, extent, shards, -0.22, 0.18) * drawn
    return jnp.clip(drawn, min=-most, max=most).astype(held_as)


def heavy_noise(own_key, dims, scale, limit, shards, heavy, held_as=jnp.bfloat16):
    entries = scale * jax.random.normal(own_key, dims, jnp.float32)
    if shards:
        entries = entries * levels(own_key, dims, shards, -0.22, 0.18)
    return jnp.clip(strengthened(entries, jax.random.fold_in(own_key, 3), *heavy), -limit, limit).astype(held_as)


def setup_inputs(seed: int = 0) -> dict:
    splits = jax.random.split(jax.random.key(seed), 6)
    query = bell_draw(splits[0], (BATCH, LENGTH, HD), 1.0, 6.0, ((0, 8), (1, 64)))
    keys = bell_draw(splits[1], (BATCH, LENGTH, HD), 1.0, 6.0, ((0, 8), (1, 64)))
    values = bell_draw(splits[2], (BATCH, LENGTH, HD), 1.0, 6.0, ((0, 8), (1, 64)))
    cotangent = heavy_noise(splits[3], (BATCH, LENGTH, D), 1.0, 16.0, ((0, 8), (1, 64)), (1, 2, 64, 4.0))
    out_weight = bell_draw(splits[4], (D, HD), D ** -0.5, 0.1875, ((0, 8),))
    return {"query": query, "keys": keys, "values": values, "cotangent": cotangent, "out_weight": out_weight}


def half_round(array):
    rounded = array.astype(jnp.bfloat16)
    return lax.optimization_barrier(rounded).astype(jnp.float32)

def reference(query, keys, values, cotangent, out_weight):
    batch_count = query.shape[0]
    seq_len = query.shape[1]
    width = query.shape[2]
    stretch = TOK_DEV
    segment_number = seq_len // stretch
    head_count = width // HEAD
    factor = 1.0 / math.sqrt(HEAD * seq_len)
    token_positions = jnp.arange(stretch, dtype=jnp.int32)
    masked_future = token_positions[:, None] >= token_positions[None, :]

    def one_sequence(operands):
        q_seq, k_seq, v_seq, dy_seq = operands
        d_out = jnp.dot(dy_seq, out_weight, preferred_element_type=jnp.float32).astype(jnp.bfloat16)
        dimensions4 = (segment_number, stretch, head_count, HEAD)
        q_all = q_seq.reshape(dimensions4).astype(jnp.float32)
        k_all = k_seq.reshape(dimensions4).astype(jnp.float32)
        v_all = v_seq.reshape(dimensions4).astype(jnp.float32)
        o_all = d_out.reshape(dimensions4).astype(jnp.float32)
        running_state_list = jnp.einsum('nchk,nchv->nhkv', k_all, v_all)
        state_gradient_list = jnp.einsum('nchk,nchv->nhkv', q_all, o_all)
        prior = jnp.cumsum(running_state_list, 0) - running_state_list
        later = jnp.cumsum(state_gradient_list[::-1], 0)[::-1] - state_gradient_list
        first_half_rows = half_round(prior)
        latter_portion_tokens = half_round(later)
        raw_scores = jnp.einsum('nthd,nshd->nhts', q_all, k_all)
        scores = half_round(jnp.where(masked_future, factor * raw_scores, 0.0))
        output = jnp.einsum('nhts,nshv->nthv', scores, v_all) + factor * jnp.einsum('nthk,nhkv->nthv', q_all, first_half_rows)
        output = output.reshape(seq_len, width).astype(jnp.bfloat16)
        raw_grad = jnp.einsum('nthv,nshv->nhts', o_all, v_all)
        score_grad = half_round(jnp.where(masked_future, factor * raw_grad, 0.0))
        q_grad = jnp.einsum('nhts,nshk->nthk', score_grad, k_all) + factor * jnp.einsum('nthv,nhkv->nthk', o_all, first_half_rows)
        k_grad = jnp.einsum('nhts,nthk->nshk', score_grad, q_all) + factor * jnp.einsum('nshv,nhkv->nshk', v_all, latter_portion_tokens)
        v_grad = jnp.einsum('nhts,nthv->nshv', scores, o_all) + factor * jnp.einsum('nshk,nhkv->nshv', k_all, latter_portion_tokens)
        weight_part = jnp.dot(dy_seq.T, output, preferred_element_type=jnp.float32)
        return (q_grad.reshape(seq_len, width).astype(jnp.bfloat16), k_grad.reshape(seq_len, width).astype(jnp.bfloat16), v_grad.reshape(seq_len, width).astype(jnp.bfloat16), weight_part)
    results = lax.map(one_sequence, (query, keys, values, cotangent))
    weight_grad = lax.optimization_barrier(jnp.sum(results[3], 0)) * (1.0 / math.sqrt(batch_count * seq_len))
    return (results[0], results[1], results[2], weight_grad)
```

```python
import functools
import math

import jax
import jax.numpy as jnp
from jax import lax
from jax.experimental import pallas as pl
from jax.experimental.pallas import tpu as pltpu
from jax.sharding import Mesh, PartitionSpec as P

HEAD = 128
F32 = jnp.float32
BF16 = jnp.bfloat16


def dot(a, b, contract):
    return lax.dot_general(a, b, ((contract[:1], contract[1:]), ((), ())), preferred_element_type=F32)


def head(ref, h):
    return ref[:, h * HEAD : (h + 1) * HEAD]


def call(kernel, core, ins, outs, **cost):
    def spec(operand):
        if isinstance(operand, tuple):
            rows, columns = operand[0].shape
            return pl.BlockSpec((rows, columns // 2), lambda i, c: (0, c[0]))
        return pl.BlockSpec(operand.shape, lambda i, c, n=operand.ndim: (0,) * n)

    arrays = [operand[0] if isinstance(operand, tuple) else operand for operand in ins]
    return pl.pallas_call(
        kernel,
        grid_spec=pltpu.PrefetchScalarGridSpec(
            num_scalar_prefetch=1,
            grid=(1,),
            in_specs=[spec(operand) for operand in ins],
            out_specs=[pl.BlockSpec(o.shape, lambda i, c, n=len(o.shape): (0,) * n) for o in outs],
        ),
        out_shape=outs,
        compiler_params=pltpu.CompilerParams(vmem_limit_bytes=48 * 1024 * 1024),
    )(core, *arrays)


def shape(dims, dtype):
    return jax.ShapeDtypeStruct(dims, dtype)


def states_kernel(core, k, v, kv_far, near, far, both):
    for h in range(near.shape[0]):
        mine = dot(head(k, h), head(v, h), (0, 0))
        other = dot(head(kv_far.at[0], h), head(kv_far.at[1], h), (0, 0))
        near[h] = mine
        far[h] = other
        both[h] = (mine + other).astype(BF16)


def prefix_kernel(reverse, core, terms, sums):
    count = terms.shape[0]
    total = jnp.zeros(terms.shape[1:], F32)
    for k in reversed(range(count)) if reverse else range(count):
        sums[k] = total.astype(BF16)
        total = total + terms[k].astype(F32)


def masked(scores, factor):
    rows = lax.broadcasted_iota(jnp.int32, scores.shape, 0)
    columns = lax.broadcasted_iota(jnp.int32, scores.shape, 1)
    return jnp.where(rows >= columns, factor * scores, 0.0).astype(BF16)


def entering(chunk, inside, here):
    return (chunk.astype(F32) + jnp.where(here, inside, 0.0)).astype(BF16)


def output_kernel(factor, core, q, k, v, q_far, kv_far, dy, dy_far, prior, s_near, s_far, weight, out, out_far):
    for h in range(s_near.shape[0]):
        for qs, ks, vs, inside, here, o in (
            (q, k, v, s_far, core[0] == 1, out),
            (q_far, kv_far.at[0], kv_far.at[1], s_near, core[0] == 0, out_far),
        ):
            qh = head(qs, h)
            before = entering(prior[h], inside[h], here)
            scores = masked(dot(qh, head(ks, h), (1, 1)), factor)
            o[:, h * HEAD : (h + 1) * HEAD] = (
                dot(scores, head(vs, h), (1, 0)) + factor * dot(qh, before, (1, 0))
            ).astype(BF16)
    weight[...] = (dot(dy[...], out[...], (0, 0)) + dot(dy_far[...], out_far[...], (0, 0))).astype(BF16)


def d_out_kernel(core, dy, dy_far, w, q, q_far, d, d_far, near, far, both):
    d[...] = dot(dy[...], w[...], (1, 0)).astype(BF16)
    d_far[...] = dot(dy_far[...], w[...], (1, 0)).astype(BF16)
    for h in range(near.shape[0]):
        mine = dot(head(q, h), head(d, h), (0, 0))
        other = dot(head(q_far, h), head(d_far, h), (0, 0))
        near[h] = mine
        far[h] = other
        both[h] = (mine + other).astype(BF16)


def grads_kernel(
    factor, core, q, k, v, q_far, kv_far, d, d_far, prior, s_near, s_far, later, g_near, g_far, near, far
):
    first = core[0] == 0
    for h in range(s_near.shape[0]):
        at = slice(h * HEAD, (h + 1) * HEAD)
        for qs, ks, vs, ds, s_in, s_here, g_in, g_here, o in (
            (q, k, v, d, s_far, core[0] == 1, g_far, first, near),
            (q_far, kv_far.at[0], kv_far.at[1], d_far, s_near, first, g_near, core[0] == 1, far),
        ):
            qh, kh, vh, dh = head(qs, h), head(ks, h), head(vs, h), head(ds, h)
            before = entering(prior[h], s_in[h], s_here)
            after = entering(later[h], g_in[h], g_here)
            scores = masked(dot(qh, kh, (1, 1)), factor)
            score_grad = masked(dot(dh, vh, (1, 1)), factor)
            o[0, :, at] = (dot(score_grad, kh, (1, 0)) + factor * dot(dh, before, (1, 1))).astype(BF16)
            o[1, :, at] = (dot(score_grad, qh, (0, 0)) + factor * dot(vh, after, (1, 1))).astype(BF16)
            o[2, :, at] = (dot(scores, dh, (0, 0)) + factor * dot(kh, after, (1, 0))).astype(BF16)


def join_kernel(core, near, far, q_grad, k_grad, v_grad):
    width = near.shape[2]
    for i, o in enumerate((q_grad, k_grad, v_grad)):

        @pl.when(core[0] == 0)
        def _():
            o[:, :width] = near[i]
            o[:, width:] = far[i]

        @pl.when(core[0] == 1)
        def _():
            o[:, :width] = far[i]
            o[:, width:] = near[i]


def sum_kernel(scale, core, parts, total):
    count, rows, columns = parts.shape
    halves = [jnp.zeros((rows, columns), F32), jnp.zeros((rows, columns), F32)]
    for k in range(count):
        halves[k % 2] = halves[k % 2] + parts[k].astype(F32)
    total[:, :columns] = halves[0] * scale
    total[:, columns:] = halves[1] * scale


def per_device(query, keys, values, cotangent, out_weight):
    q, k, v, dy = query[0], keys[0], values[0], cotangent[0]
    stretch, width = q.shape
    half = width // 2
    heads = half // HEAD
    sizes = {axis: lax.axis_size(axis) for axis in ("y", "z", "x", "c")}
    chips = sizes["z"] * sizes["x"]
    seq_len = stretch * chips * 2
    factor = 1.0 / math.sqrt(HEAD * seq_len)
    grad_factor = 1.0 / math.sqrt(sizes["y"] * seq_len)
    c = lax.axis_index("c")
    core = c.reshape(1).astype(jnp.int32)

    def halves(a, index):
        return lax.dynamic_slice_in_dim(a, index * half, half, 1)

    def swap(a):
        return lax.ppermute(a, "c", ((0, 1), (1, 0)))

    w = lax.all_gather(halves(out_weight, c), "y", axis=0, tiled=True)
    kv_far = swap(jnp.stack([halves(k, 1 - c), halves(v, 1 - c)]))
    q_dy_far = swap(jnp.concatenate([halves(q, 1 - c), dy], 1))
    q_far, dy_far = q_dy_far[:, :half], q_dy_far[:, half:]

    def scan(both, reverse):
        slices = both.reshape(chips, heads * HEAD // chips, HEAD)
        slices = lax.all_to_all(slices, ("z", "x"), 0, 0)
        (sums,) = call(functools.partial(prefix_kernel, reverse), core, [slices], [shape(slices.shape, BF16)])
        return lax.all_to_all(sums, ("z", "x"), 0, 0).reshape(heads, HEAD, HEAD)

    states = [shape((heads, HEAD, HEAD), t) for t in (F32, F32, BF16)]
    tokens = shape((stretch, half), BF16)

    s_near, s_far, s_both = call(states_kernel, core, [(k, 0), (v, 0), kv_far], states)
    prior = scan(s_both, False)
    partial, _, _ = call(
        functools.partial(output_kernel, factor),
        core,
        [(q, 0), (k, 0), (v, 0), q_far, kv_far, dy, dy_far, prior, s_near, s_far],
        [shape((width, half), BF16), tokens, tokens],
    )
    scattered = lax.psum_scatter(partial, "y", scatter_dimension=0, tiled=True)

    d, d_far, g_near, g_far, g_both = call(
        d_out_kernel, core, [dy, dy_far, w, (q, 0), q_far], [tokens, tokens] + states
    )
    later = scan(g_both, True)
    grads = shape((3, stretch, half), BF16)
    near, far = call(
        functools.partial(grads_kernel, factor),
        core,
        [(q, 0), (k, 0), (v, 0), q_far, kv_far, d, d_far, prior, s_near, s_far, later, g_near, g_far],
        [grads, grads],
    )
    back = swap(far)
    whole = shape((stretch, width), BF16)
    q_grad, k_grad, v_grad = call(join_kernel, core, [near, back], [whole] * 3)

    rows = width // sizes["y"] // (chips * 2)
    parts = lax.all_to_all(scattered.reshape(chips * 2, rows, half), ("z", "x", "c"), 0, 0)
    (weight_grad,) = call(functools.partial(sum_kernel, grad_factor), core, [parts], [shape((rows, width), F32)])
    return q_grad[None], k_grad[None], v_grad[None], weight_grad


def solution(mesh):
    dp, ctx = mesh.devices.shape
    chips = Mesh(mesh.devices.reshape(dp, ctx // 8, 4, 2), ("y", "z", "x", "c"))
    tokens = P("y", ("z", "x", "c"), None)
    return jax.shard_map(
        per_device,
        mesh=chips,
        in_specs=(tokens, tokens, tokens, tokens, P("y", None)),
        out_specs=(tokens, tokens, tokens, P(("y", "z", "x", "c"), None)),
        check_vma=False,
    )
```

```python
import functools
import math

import jax
import jax.numpy as jnp
from jax import lax
from jax.experimental import pallas as pl
from jax.experimental.pallas import tpu as pltpu
from jax.sharding import Mesh, PartitionSpec as P

HEAD = 128
F32 = jnp.float32
BF16 = jnp.bfloat16


def dot(a, b, contract):
    return lax.dot_general(a, b, ((contract[:1], contract[1:]), ((), ())), preferred_element_type=F32)


def head(ref, h):
    return ref[:, h * HEAD : (h + 1) * HEAD]


def call(kernel, core, ins, outs, scratch=(), vmem=60):
    def spec(operand):
        if isinstance(operand, tuple):
            array, columns, place = operand
            if place is None:
                return pl.BlockSpec((array.shape[0], columns), lambda i, c: (0, c[0]))
            return pl.BlockSpec((array.shape[0], columns), lambda i, c: (0, place))
        return pl.BlockSpec(operand.shape, lambda i, c, n=operand.ndim: (0,) * n)

    arrays = [operand[0] if isinstance(operand, tuple) else operand for operand in ins]
    return pl.pallas_call(
        kernel,
        grid_spec=pltpu.PrefetchScalarGridSpec(
            num_scalar_prefetch=1,
            grid=(1,),
            in_specs=[spec(operand) for operand in ins],
            out_specs=[pl.BlockSpec(o.shape, lambda i, c, n=len(o.shape): (0,) * n) for o in outs],
            scratch_shapes=scratch,
        ),
        out_shape=outs,
        compiler_params=pltpu.CompilerParams(vmem_limit_bytes=vmem * 1024 * 1024),
    )(core, *arrays)


def shape(dims, dtype):
    return jax.ShapeDtypeStruct(dims, dtype)


def masked(scores, factor):
    rows = lax.broadcasted_iota(jnp.int32, scores.shape, 0)
    columns = lax.broadcasted_iota(jnp.int32, scores.shape, 1)
    return jnp.where(rows >= columns, factor * scores, 0.0).astype(BF16)


def entering(chunk, inside, here):
    return (chunk.astype(F32) + jnp.where(here, inside, 0.0)).astype(BF16)


def local_kernel(factor, core, q, k, v, dy, far, near_state, far_state, near_out, far_out, dy_turned):
    half = q.shape[1]
    tokens = q.shape[0]
    q_far, k_far, v_far = (far.at[:, i * half : (i + 1) * half] for i in range(3))
    for h in range(near_state.shape[0]):
        at = slice(h * HEAD, (h + 1) * HEAD)
        for qs, ks, vs, state, o in ((q, k, v, near_state, near_out), (q_far, k_far, v_far, far_state, far_out)):
            qh, kh, vh = head(qs, h), head(ks, h), head(vs, h)
            state[h] = dot(kh, vh, (0, 0))
            o[:, at] = dot(masked(dot(qh, kh, (1, 1)), factor), vh, (1, 0))
    dy_turned[:, :tokens] = dy[...].T
    dy_turned[:, tokens:] = far[:, 3 * half :].T


def d_out_kernel(core, dy, far, w, q, near_state, far_state, d, d_far, near, other, both):
    half = q.shape[1]
    d[...] = dot(dy[...], w[...], (1, 0)).astype(BF16)
    d_far[...] = dot(far[:, 3 * half :], w[...], (1, 0)).astype(BF16)
    chips, lines, _ = both.shape
    lines = lines // 2
    per_head = HEAD // lines
    for h in range(near.shape[0]):
        g = dot(head(q, h), head(d, h), (0, 0))
        g_far = dot(head(far, h), head(d_far, h), (0, 0))
        near[h] = g
        other[h] = g_far
        for side, total in ((0, near_state[h] + far_state[h]), (1, g + g_far)):
            total = total.astype(BF16).reshape(per_head, lines, HEAD)
            both[h * per_head : (h + 1) * per_head, side * lines : (side + 1) * lines, :] = total


def prefix_kernel(core, terms, sums):
    count, lines, _ = terms.shape
    half = lines // 2
    for order, at in ((range(count), slice(0, half)), (reversed(range(count)), slice(half, lines))):
        total = jnp.zeros((half, HEAD), F32)
        for k in order:
            sums[k, at, :] = total.astype(BF16)
            total = total + terms[k, at, :].astype(F32)


def chunk_sum(sums, h, side):
    _, lines, _ = sums.shape
    lines = lines // 2
    per_head = HEAD // lines
    return sums[h * per_head : (h + 1) * per_head, side * lines : (side + 1) * lines, :].reshape(HEAD, HEAD)


def output_kernel(factor, core, q, far, sums, s_near, s_far, local, local_far, dy_turned, weight, out, held):
    tokens = q.shape[0]
    for h in range(s_near.shape[0]):
        at = slice(h * HEAD, (h + 1) * HEAD)
        prior = chunk_sum(sums, h, 0)
        for qs, inside, here, part, rows in (
            (q, s_far, core[0] == 1, local, slice(0, tokens)),
            (far, s_near, core[0] == 0, local_far, slice(tokens, 2 * tokens)),
        ):
            before = entering(prior, inside[h], here)
            out[rows, at] = (part[:, at] + factor * dot(head(qs, h), before, (1, 0))).astype(BF16)
    whole = dot(dy_turned[...], out[...], (1, 0))
    for b in range(s_near.shape[0]):
        held[b] = whole[:, b * HEAD : (b + 1) * HEAD]
    places, lines, count, _ = weight.shape
    for x in range(places):
        for t in range(lines):
            for b in range(s_near.shape[0]):
                at = slice(b * HEAD, (b + 1) * HEAD)
                weight[x, t, :, at] = held[b, pl.ds(x * lines + t, count, stride=places * lines), :].astype(BF16)


def grads_kernel(factor, core, q, k, v, far, d, d_far, sums, s_near, s_far, g_near, g_far, near, other):
    first = core[0] == 0
    half = q.shape[1]
    q_far, k_far, v_far = (far.at[:, i * half : (i + 1) * half] for i in range(3))
    for h in range(s_near.shape[0]):
        at = slice(h * HEAD, (h + 1) * HEAD)
        prior, later = chunk_sum(sums, h, 0), chunk_sum(sums, h, 1)
        for qs, ks, vs, ds, s_in, s_here, g_in, g_here, o in (
            (q, k, v, d, s_far, core[0] == 1, g_far, first, near),
            (q_far, k_far, v_far, d_far, s_near, first, g_near, core[0] == 1, other),
        ):
            qh, kh, vh, dh = head(qs, h), head(ks, h), head(vs, h), head(ds, h)
            before = entering(prior, s_in[h], s_here)
            after = entering(later, g_in[h], g_here)
            scores = masked(dot(qh, kh, (1, 1)), factor)
            score_grad = masked(dot(dh, vh, (1, 1)), factor)
            o[0, :, at] = (dot(score_grad, kh, (1, 0)) + factor * dot(dh, before, (1, 1))).astype(BF16)
            o[1, :, at] = (dot(score_grad, qh, (0, 0)) + factor * dot(vh, after, (1, 1))).astype(BF16)
            o[2, :, at] = (dot(scores, dh, (0, 0)) + factor * dot(kh, after, (1, 0))).astype(BF16)


def join_kernel(core, near, far, q_grad, k_grad, v_grad):
    width = near.shape[2]
    for i, o in enumerate((q_grad, k_grad, v_grad)):

        @pl.when(core[0] == 0)
        def _():
            o[:, :width] = near[i]
            o[:, width:] = far[i]

        @pl.when(core[0] == 1)
        def _():
            o[:, :width] = far[i]
            o[:, width:] = near[i]


def gather_rows_kernel(core, parts, lines, held):
    places, rows, count, columns = parts.shape
    blocks = columns // HEAD
    for t in range(rows):
        for b in range(blocks):
            total = jnp.zeros((count, HEAD), F32)
            for x in range(places):
                total = total + parts[x, t, :, b * HEAD : (b + 1) * HEAD].astype(F32)
            held[pl.ds(t * blocks + b, count, stride=rows * blocks), :] = total
    lines[...] = held[...].astype(BF16)


def sum_kernel(scale, core, parts, total, held):
    count, lines, _ = parts.shape
    rows, width = total.shape
    blocks = lines // rows
    for side in range(2):
        added = jnp.zeros((lines, HEAD), F32)
        for k in range(side, count, 2):
            added = added + parts[k].astype(F32)
        held[...] = added * scale
        for b in range(blocks):
            at = side * blocks * HEAD + b * HEAD
            total[:, at : at + HEAD] = held[pl.ds(b, rows, stride=blocks), :]


def per_device(query, keys, values, cotangent, out_weight):
    q, k, v, dy = query[0], keys[0], values[0], cotangent[0]
    stretch, width = q.shape
    half = width // 2
    heads = half // HEAD
    sizes = {axis: lax.axis_size(axis) for axis in ("y", "z", "x", "c")}
    chips = sizes["z"] * sizes["x"]
    seq_len = stretch * chips * 2
    factor = 1.0 / math.sqrt(HEAD * seq_len)
    grad_factor = 1.0 / math.sqrt(sizes["y"] * seq_len)
    c = lax.axis_index("c")
    core = c.reshape(1).astype(jnp.int32)

    def halves(a, index):
        return lax.dynamic_slice_in_dim(a, index * half, half, 1)

    def swap(a):
        return lax.ppermute(a, "c", ((0, 1), (1, 0)))

    copies = jnp.broadcast_to(halves(out_weight, c)[None], (sizes["y"], width // sizes["y"], half))
    w = lax.all_to_all(copies, "y", 0, 0).reshape(width, half)
    far = swap(jnp.concatenate([halves(q, 1 - c), halves(k, 1 - c), halves(v, 1 - c), dy], 1))
    own = [(a, half, None) for a in (q, k, v)]

    state = shape((heads, HEAD, HEAD), F32)
    tokens = shape((stretch, half), BF16)
    part = shape((stretch, half), F32)
    s_near, s_far, local, local_far, dy_turned = call(
        functools.partial(local_kernel, factor),
        core,
        own + [dy, far],
        [state, state, part, part, shape((width, 2 * stretch), BF16)],
    )
    slices = shape((chips, 2 * heads * HEAD // chips, HEAD), BF16)
    d, d_far, g_near, g_far, both = call(
        d_out_kernel, core, [dy, far, w, own[0], s_near, s_far], [tokens, tokens, state, state, slices]
    )
    both = lax.all_to_all(both, ("z", "x"), 0, 0)
    (sums,) = call(prefix_kernel, core, [both], [slices])
    sums = lax.all_to_all(sums, ("z", "x"), 0, 0)

    rows = width // sizes["y"] // (chips * 2)
    blocks = half // HEAD
    places = sizes["y"] * sizes["z"]
    partial, _ = call(
        functools.partial(output_kernel, factor),
        core,
        [own[0], far, sums, s_near, s_far, local, local_far, dy_turned],
        [shape((sizes["x"], 2 * rows, places, half), BF16), shape((2 * stretch, half), BF16)],
        [pltpu.VMEM((blocks, width, HEAD), F32)],
    )
    parts = lax.all_to_all(partial, "x", 0, 0)

    grads = shape((3, stretch, half), BF16)
    near, other = call(
        functools.partial(grads_kernel, factor),
        core,
        own + [far, d, d_far, sums, s_near, s_far, g_near, g_far],
        [grads, grads],
    )
    back = swap(other)
    whole = shape((stretch, width), BF16)
    q_grad, k_grad, v_grad = call(join_kernel, core, [near, back], [whole] * 3)

    lines = shape((places * 2 * rows * blocks, HEAD), BF16)
    (summed,) = call(gather_rows_kernel, core, [parts], [lines], [pltpu.VMEM(lines.shape, F32)])
    summed = lax.all_to_all(summed.reshape(places * 2, rows * blocks, HEAD), ("y", "z", "c"), 0, 0)
    (weight_grad,) = call(
        functools.partial(sum_kernel, grad_factor),
        core,
        [summed],
        [shape((rows, width), F32)],
        [pltpu.VMEM((rows * blocks, HEAD), F32)],
    )
    return q_grad[None], k_grad[None], v_grad[None], weight_grad


def solution(mesh):
    dp, ctx = mesh.devices.shape
    chips = Mesh(mesh.devices.reshape(dp, ctx // 8, 4, 2), ("y", "z", "x", "c"))
    tokens = P("y", ("z", "x", "c"), None)
    return jax.shard_map(
        per_device,
        mesh=chips,
        in_specs=(tokens, tokens, tokens, tokens, P("y", None)),
        out_specs=(tokens, tokens, tokens, P(("y", "z", "x", "c"), None)),
        check_vma=False,
    )
```

```python
import functools
import math

import jax
import jax.numpy as jnp
from jax import lax
from jax.experimental import pallas as pl
from jax.experimental.pallas import tpu as pltpu
from jax.sharding import Mesh, PartitionSpec as P

HEAD = 128
F32 = jnp.float32
BF16 = jnp.bfloat16


def dot(a, b, contract):
    return lax.dot_general(a, b, ((contract[:1], contract[1:]), ((), ())), preferred_element_type=F32)


def head(ref, h):
    return ref[:, h * HEAD : (h + 1) * HEAD]


def call(kernel, core, ins, outs, scratch=(), vmem=16):
    def spec(operand):
        if isinstance(operand, tuple):
            array, columns, place = operand
            if place is None:
                return pl.BlockSpec((array.shape[0], columns), lambda i, c: (0, c[0]))
            return pl.BlockSpec((array.shape[0], columns), lambda i, c: (0, place))
        return pl.BlockSpec(operand.shape, lambda i, c, n=operand.ndim: (0,) * n)

    arrays = [operand[0] if isinstance(operand, tuple) else operand for operand in ins]
    return pl.pallas_call(
        kernel,
        grid_spec=pltpu.PrefetchScalarGridSpec(
            num_scalar_prefetch=1,
            grid=(1,),
            in_specs=[spec(operand) for operand in ins],
            out_specs=[pl.BlockSpec(o.shape, lambda i, c, n=len(o.shape): (0,) * n) for o in outs],
            scratch_shapes=scratch,
        ),
        out_shape=outs,
        compiler_params=pltpu.CompilerParams(vmem_limit_bytes=vmem * 1024 * 1024),
    )(core, *arrays)


def shape(dims, dtype):
    return jax.ShapeDtypeStruct(dims, dtype)


def masked(scores, factor):
    rows = lax.broadcasted_iota(jnp.int32, scores.shape, 0)
    columns = lax.broadcasted_iota(jnp.int32, scores.shape, 1)
    return jnp.where(rows >= columns, factor * scores, 0.0).astype(BF16)


def entering(chunk, inside, here):
    return (chunk.astype(F32) + jnp.where(here, inside, 0.0)).astype(BF16)


def copies_kernel(core, w, copies):
    for k in range(copies.shape[0]):
        copies[k] = w[...]


def local_kernel(factor, core, q, k, v, dy, dy_far, q_far, k_far, v_far, inside, both, out, out_far, dy_turned):
    tokens = q.shape[0]
    for h in range(inside.shape[0]):
        at = slice(h * HEAD, (h + 1) * HEAD)
        states = []
        for qs, ks, vs, o in ((q, k, v, out), (q_far, k_far, v_far, out_far)):
            qh, kh, vh = head(qs, h), head(ks, h), head(vs, h)
            states.append(dot(kh, vh, (0, 0)))
            o[:, at] = dot(masked(dot(qh, kh, (1, 1)), factor), vh, (1, 0))
        inside[h] = jnp.where(core[0] == 0, states[0], states[1])
        both[h] = (states[0] + states[1]).astype(BF16)
    dy_turned[:, :tokens] = dy[...].T
    dy_turned[:, tokens:] = dy_far[...].T


def d_out_kernel(core, dy, dy_far, w, q, q_far, states, d, d_far, inside, both):
    d[...] = dot(dy[...], w[...], (1, 0)).astype(BF16)
    d_far[...] = dot(dy_far[...], w[...], (1, 0)).astype(BF16)
    _, lines, _ = both.shape
    lines = lines // 2
    per_head = HEAD // lines
    for h in range(inside.shape[0]):
        g = dot(head(q, h), head(d, h), (0, 0))
        g_far = dot(head(q_far, h), head(d_far, h), (0, 0))
        inside[h] = jnp.where(core[0] == 0, g_far, g)
        for side, total in ((0, states[h]), (1, (g + g_far).astype(BF16))):
            total = total.reshape(per_head, lines, HEAD)
            both[h * per_head : (h + 1) * per_head, side * lines : (side + 1) * lines, :] = total


def prefix_kernel(core, terms, sums):
    count, lines, _ = terms.shape
    half = lines // 2
    for order, at in ((range(count), slice(0, half)), (reversed(range(count)), slice(half, lines))):
        total = jnp.zeros((half, HEAD), F32)
        for k in order:
            sums[k, at, :] = total.astype(BF16)
            total = total + terms[k, at, :].astype(F32)


def chunk_sum(sums, h, side):
    _, lines, _ = sums.shape
    lines = lines // 2
    per_head = HEAD // lines
    return sums[h * per_head : (h + 1) * per_head, side * lines : (side + 1) * lines, :].reshape(HEAD, HEAD)


def output_kernel(factor, core, q, q_far, sums, s_in, local, local_far, dy_turned, weight, out, held):
    tokens = q.shape[0]
    for h in range(s_in.shape[0]):
        at = slice(h * HEAD, (h + 1) * HEAD)
        prior = chunk_sum(sums, h, 0)
        for side, (qs, part) in enumerate(((q, local), (q_far, local_far))):
            before = entering(prior, s_in[h], core[0] == 1 - side)
            whole = part[:, at] + factor * dot(head(qs, h), before, (1, 0))
            out[side * tokens : (side + 1) * tokens, at] = whole.astype(BF16)
    whole = dot(dy_turned[...], out[...], (1, 0))
    for b in range(s_in.shape[0]):
        held[b] = whole[:, b * HEAD : (b + 1) * HEAD]
    places, lines, count, _ = weight.shape
    for x in range(places):
        for t in range(lines):
            for b in range(s_in.shape[0]):
                at = slice(b * HEAD, (b + 1) * HEAD)
                weight[x, t, :, at] = held[b, pl.ds(x * lines + t, count, stride=places * lines), :].astype(BF16)


def grads_kernel(factor, core, q, k, v, q_far, k_far, v_far, d, d_far, sums, s_in, g_in, near, other):
    for h in range(s_in.shape[0]):
        at = slice(h * HEAD, (h + 1) * HEAD)
        prior, later = chunk_sum(sums, h, 0), chunk_sum(sums, h, 1)
        for side, (qs, ks, vs, ds, o) in enumerate(((q, k, v, d, near), (q_far, k_far, v_far, d_far, other))):
            qh, kh, vh, dh = head(qs, h), head(ks, h), head(vs, h), head(ds, h)
            before = entering(prior, s_in[h], core[0] == 1 - side)
            after = entering(later, g_in[h], core[0] == side)
            scores = masked(dot(qh, kh, (1, 1)), factor)
            score_grad = masked(dot(dh, vh, (1, 1)), factor)
            o[0, :, at] = (dot(score_grad, kh, (1, 0)) + factor * dot(dh, before, (1, 1))).astype(BF16)
            o[1, :, at] = (dot(score_grad, qh, (0, 0)) + factor * dot(vh, after, (1, 1))).astype(BF16)
            o[2, :, at] = (dot(scores, dh, (0, 0)) + factor * dot(kh, after, (1, 0))).astype(BF16)


def join_kernel(core, near, far, q_grad, k_grad, v_grad):
    width = near.shape[2]
    for i, o in enumerate((q_grad, k_grad, v_grad)):

        @pl.when(core[0] == 0)
        def _():
            o[:, :width] = near[i]
            o[:, width:] = far[i]

        @pl.when(core[0] == 1)
        def _():
            o[:, :width] = far[i]
            o[:, width:] = near[i]


def gather_rows_kernel(core, parts, lines, held):
    places, rows, count, columns = parts.shape
    blocks = columns // HEAD
    for t in range(rows):
        for b in range(blocks):
            total = jnp.zeros((count, HEAD), F32)
            for x in range(places):
                total = total + parts[x, t, :, b * HEAD : (b + 1) * HEAD].astype(F32)
            held[pl.ds(t * blocks + b, count, stride=rows * blocks), :] = total
    lines[...] = held[...].astype(BF16)


def sum_kernel(scale, core, parts, total, held):
    count, lines, _ = parts.shape
    rows, width = total.shape
    blocks = lines // rows
    for side in range(2):
        added = jnp.zeros((lines, HEAD), F32)
        for k in range(side, count, 2):
            added = added + parts[k].astype(F32)
        held[...] = added * scale
        for b in range(blocks):
            at = side * blocks * HEAD + b * HEAD
            total[:, at : at + HEAD] = held[pl.ds(b, rows, stride=blocks), :]


def per_device(query, keys, values, cotangent, out_weight):
    q, k, v, dy = query[0], keys[0], values[0], cotangent[0]
    stretch, width = q.shape
    half = width // 2
    heads = half // HEAD
    sizes = {axis: lax.axis_size(axis) for axis in ("y", "z", "x", "c")}
    chips = sizes["z"] * sizes["x"]
    seq_len = stretch * chips * 2
    factor = 1.0 / math.sqrt(HEAD * seq_len)
    grad_factor = 1.0 / math.sqrt(sizes["y"] * seq_len)
    c = lax.axis_index("c")
    core = c.reshape(1).astype(jnp.int32)

    def halves(a, index):
        return lax.dynamic_slice_in_dim(a, index * half, half, 1)

    def swap(a):
        return lax.ppermute(a, "c", ((0, 1), (1, 0)))

    (copies,) = call(
        copies_kernel, core, [(out_weight, half, None)], [shape((sizes["y"], width // sizes["y"], half), BF16)], vmem=60
    )
    w = lax.all_to_all(copies, "y", 0, 0).reshape(width, half)
    far = swap(jnp.concatenate([dy, halves(q, 1 - c), halves(k, 1 - c), halves(v, 1 - c)], 1))
    own = [(a, half, None) for a in (q, k, v)]
    dy_far = (far, width, 0)
    others = [(far, half, width // half + i) for i in range(3)]

    inside = shape((heads, HEAD, HEAD), F32)
    tokens = shape((stretch, half), BF16)
    part = shape((stretch, half), F32)
    s_in, s_both, local, local_far, dy_turned = call(
        functools.partial(local_kernel, factor),
        core,
        own + [dy, dy_far] + others,
        [inside, shape(inside.shape, BF16), part, part, shape((width, 2 * stretch), BF16)],
        vmem=24,
    )
    slices = shape((chips, 2 * heads * HEAD // chips, HEAD), BF16)
    d, d_far, g_in, both = call(
        d_out_kernel, core, [dy, dy_far, w, own[0], others[0], s_both], [tokens, tokens, inside, slices], vmem=16
    )
    both = lax.all_to_all(both, ("z", "x"), 0, 0)
    (sums,) = call(prefix_kernel, core, [both], [slices], vmem=3)
    sums = lax.all_to_all(sums, ("z", "x"), 0, 0)

    rows = width // sizes["y"] // (chips * 2)
    blocks = half // HEAD
    places = sizes["y"] * sizes["z"]
    partial, _ = call(
        functools.partial(output_kernel, factor),
        core,
        [own[0], others[0], sums, s_in, local, local_far, dy_turned],
        [shape((sizes["x"], 2 * rows, places, half), BF16), shape((2 * stretch, half), BF16)],
        [pltpu.VMEM((blocks, width, HEAD), F32)],
        vmem=24,
    )
    parts = lax.all_to_all(partial, "x", 0, 0)

    grads = shape((3, stretch, half), BF16)
    near, other = call(
        functools.partial(grads_kernel, factor),
        core,
        own + others + [d, d_far, sums, s_in, g_in],
        [grads, grads],
        vmem=60,
    )
    back = swap(other)
    whole = shape((stretch, width), BF16)
    q_grad, k_grad, v_grad = call(join_kernel, core, [near, back], [whole] * 3, vmem=10)

    lines = shape((places * 2 * rows * blocks, HEAD), BF16)
    (summed,) = call(gather_rows_kernel, core, [parts], [lines], [pltpu.VMEM(lines.shape, F32)], vmem=8)
    summed = lax.all_to_all(summed.reshape(places * 2, rows * blocks, HEAD), ("y", "z", "c"), 0, 0)
    (weight_grad,) = call(
        functools.partial(sum_kernel, grad_factor),
        core,
        [summed],
        [shape((rows, width), F32)],
        [pltpu.VMEM((rows * blocks, HEAD), F32)],
        vmem=3,
    )
    return q_grad[None], k_grad[None], v_grad[None], weight_grad


def solution(mesh):
    dp, ctx = mesh.devices.shape
    chips = Mesh(mesh.devices.reshape(dp, ctx // 8, 4, 2), ("y", "z", "x", "c"))
    tokens = P("y", ("z", "x", "c"), None)
    return jax.shard_map(
        per_device,
        mesh=chips,
        in_specs=(tokens, tokens, tokens, tokens, P("y", None)),
        out_specs=(tokens, tokens, tokens, P(("y", "z", "x", "c"), None)),
        check_vma=False,
    )
```
